32 devices in a mesh: groups: 2 (over y), dp: 4 (over x, core), tensor: 4 (over z).
Axes of the slice: x: 2, y: 2, z: 4, core: 2. Of those that a mesh axis runs over, the one named last changes fastest.
Arguments:
- gate_pre: bfloat16 [4096, 13824], P(('groups', 'dp'), 'tensor'), parts along dimension 0, may hold values from -6 to 6
- up_pre: bfloat16 [4096, 13824], P(('groups', 'dp'), 'tensor'), parts along dimension 0, may hold values from -6 to 6
- d_out: bfloat16 [4096, 5120], P(('groups', 'dp'), 'tensor'), parts along dimension 0, may hold values from -6 to 6
- lengths: int32 [32], P(('groups', 'dp')), parts along dimension 0, may hold values from 1 to 128, 1280 in all
- w_gate: bfloat16 [5120, 13824], P('dp', 'tensor'), may hold values from -0.0546875 to 0.0546875
- w_up: bfloat16 [5120, 13824], P('dp', 'tensor'), may hold values from -0.0546875 to 0.0546875
- w_down: bfloat16 [13824, 5120], P('tensor', 'dp'), may hold values from -0.078125 to 0.078125
- buckets_ff: int32 [13824], P('tensor'), may hold values from 0 to 255
- signs_ff: int32 [13824], P('tensor'), may hold values from 0 to 1
- buckets_d: int32 [5120], replicated, may hold values from 0 to 255
- signs_d: int32 [5120], replicated, may hold values from 0 to 1
- queries: bfloat16 [4096, 65536], P('dp', 'tensor'), may hold values from -6 to 6
Outputs:
- grad_input: bfloat16 [4096, 5120], P(('groups', 'dp'), 'tensor'), parts along dimension 0
- scores: float32 [8192, 16], P(('groups', 'dp')), parts along dimension 0
The draws below stay inside these ranges and needn't reach their ends.
There are 2 independent parts, one for each index of `groups`. The reference program is written for one: setup_inputs(seed, part) draws one part's arguments, and reference() takes and returns one part's arrays. A program takes and returns all parts, laid end to end along the dimension named above; an argument that names none is the same for every part. Nothing has to cross between parts.
Inputs may be any that keep to these rules, and one draw needn't show every extreme that they name: The 4 lengths of each index of dp sum to at most 512; in each part along groups all lengths sum to 1280; the largest in each part is exactly 128.
All inputs are finite; a program needn't handle non-finite values.
Results may differ from the reference program's by a relative error of at most 0.0095.
Values may be sent and summed in bfloat16 or wider, within the bound.
A program may use at most 384 MiB of HBM per device.

```python
import math
import jax
import jax.numpy as jnp
import numpy as np
from jax import lax

D = 5120
FF = 13824
SK = 256
EX_DEV = 4
TOK_DEV = 512
TOKENS = 2048
EXAMPLES = 16
QUERIES = 4096
N_DP = 4
N_TENSOR = 4


def touch_ends(result, rng, low, largest):
    spot = [jax.random.randint(jax.random.fold_in(rng, axis), (), 0, length) for axis, length in enumerate(result.shape)]
    main_axis = result.shape.index(max(result.shape))
    beside = spot[:main_axis] + [(spot[main_axis] + 1) % result.shape[main_axis]] + spot[main_axis + 1:]
    return result.at[tuple(spot)].set(low).at[tuple(beside)].set(largest)


def level_of(stream_key, extent, cuts, low, largest):
    def one(position, blocks):
        heights = jax.random.uniform(jax.random.fold_in(jax.random.fold_in(stream_key, 6), position), (blocks,), jnp.float32, low / len(cuts), largest / len(cuts))
        return jnp.repeat(jnp.exp(heights), extent[position] // blocks).reshape((-1,) + (1,) * (len(extent) - position - 1))

    factor_of = one(*cuts[0])
    for cut in cuts[1:]:
        factor_of = factor_of * one(*cut)
    return factor_of


def profile(amount, total, reach, skew):
    weights = [(1 << 20) // math.isqrt(standing ** skew) + 1 for standing in range(2, amount + 1)]
    rest, holding = total - reach - (amount - 1), [1] * (amount - 1)
    while rest > 0:
        movable = [i for i in range(amount - 1) if holding[i] < reach]
        mass, left = sum([weights[i] for i in movable]), rest
        for i in movable:
            addition = min(reach - holding[i], max(1, left * weights[i] // mass), rest)
            holding[i] = holding[i] + addition
            rest = rest - addition
    return np.array([reach] + holding)


def ragged(rng, count, total, bound, lean):
    if count == 2:
        one = jax.random.randint(rng, (), max(1, total - bound), min(bound, total - 1) + 1)
        return jnp.stack([one, total - one])
    sizes = jnp.asarray(profile(count, total, bound, lean), jnp.int32)
    couples = (count - 1) // 2
    source_of, sink = sizes[1:1 + 2 * couples:2], sizes[2:2 + 2 * couples:2]
    margin = jnp.minimum(source_of - 1, bound - sink)
    passed = jax.random.randint(jax.random.fold_in(rng, 1), (couples,), 0, 1 << 20) % (margin + 1)
    sizes = sizes.at[1:1 + 2 * couples:2].set(source_of - passed).at[2:2 + 2 * couples:2].set(sink + passed)
    return sizes[jax.random.permutation(jax.random.fold_in(rng, 2), count)]


def normal_values(rng, dims, scale, limit, split=(), kind=jnp.bfloat16):
    gain = level_of(rng, dims, split, -0.22, 0.18) if split else 1.0
    values = jax.random.normal(rng, dims, jnp.float32) * scale * gain
    return jnp.minimum(jnp.maximum(values, -limit), limit).astype(kind)


def setup_inputs(seed: int = 0, part: int = 0) -> dict:
    keys = jax.random.split(jax.random.key(seed), 13)
    part_splits = jax.random.split(jax.random.fold_in(keys[12], part), 13)
    return {
        "gate_pre": normal_values(part_splits[0], (TOKENS, FF), 1.0, 6.0, ((0, 4), (1, 4))),
        "up_pre": normal_values(part_splits[1], (TOKENS, FF), 1.0, 6.0, ((0, 4), (1, 4))),
        "d_out": normal_values(part_splits[2], (TOKENS, D), 1.0, 6.0, ((0, 4), (1, 4))),
        "lengths": ragged(part_splits[3], EXAMPLES, EXAMPLES * TOK_DEV * 5 // 32, TOK_DEV // 4, 2).astype(jnp.int32),
        "w_gate": normal_values(keys[4], (D, FF), FF ** -0.5, 0.0546875, ((0, 4), (1, 4))),
        "w_up": normal_values(keys[5], (D, FF), FF ** -0.5, 0.0546875, ((0, 4), (1, 4))),
        "w_down": normal_values(keys[6], (FF, D), D ** -0.5, 0.078125, ((0, 4), (1, 4))),
        "buckets_ff": touch_ends(jax.random.randint(keys[7], (FF,), 0, SK), jax.random.fold_in(keys[7], 1), 0, SK - 1).astype(jnp.int32),
        "signs_ff": touch_ends(jax.random.randint(keys[8], (FF,), 0, 2), jax.random.fold_in(keys[8], 1), 0, 1).astype(jnp.int32),
        "buckets_d": touch_ends(jax.random.randint(keys[9], (D,), 0, SK), jax.random.fold_in(keys[9], 1), 0, SK - 1).astype(jnp.int32),
        "signs_d": touch_ends(jax.random.randint(keys[10], (D,), 0, 2), jax.random.fold_in(keys[10], 1), 0, 1).astype(jnp.int32),
        "queries": normal_values(keys[11], (QUERIES, SK * SK), 1.0, 6.0, ((0, 4), (1, 4))),
    }


def membership(lengths):
    lens = lengths.reshape(N_DP, EX_DEV)
    finish = jnp.cumsum(lens, axis=1)
    starts = finish - lens
    row_ids = jnp.arange(TOKENS, dtype=jnp.int32)
    owner = row_ids // TOK_DEV
    local = row_ids % TOK_DEV
    ex_ids = jnp.arange(EXAMPLES, dtype=jnp.int32)
    same = owner[:, None] == (ex_ids // EX_DEV)[None, :]
    inside = (local[:, None] >= starts.reshape(-1)[None, :]) & (local[:, None] < finish.reshape(-1)[None, :])
    return (same & inside).astype(jnp.float32)

def sign_table(buckets, signs):
    hits = buckets[:, None] == jnp.arange(SK, dtype=jnp.int32)[None, :]
    values = (2 * signs - 1).astype(jnp.float32)[:, None]
    return jnp.where(hits, values, jnp.float32(0.0)).astype(jnp.bfloat16)

def contract_last(left, right):
    return lax.dot_general(left, right, (((1,), (1,)), ((), ())), preferred_element_type=jnp.float32)

def reference(gate_pre, up_pre, d_out, lengths, w_gate, w_up, w_down, buckets_ff, signs_ff, buckets_d, signs_d, queries):
    member = membership(lengths)
    live_rows = lax.optimization_barrier(jnp.sum(member, axis=1))
    d_live = jnp.where(live_rows[:, None] > 0, d_out, jnp.zeros_like(d_out))
    grad_hidden = jnp.dot(d_live, w_down.T, preferred_element_type=jnp.float32)
    gate_val = gate_pre.astype(jnp.float32)
    up_val = up_pre.astype(jnp.float32)
    sigmoid_gate = jax.nn.sigmoid(gate_val)
    silu_gate = gate_val * sigmoid_gate
    hidden = (silu_gate * up_val).astype(jnp.bfloat16)
    grad_gate = (grad_hidden * up_val * sigmoid_gate * (1.0 + gate_val * (1.0 - sigmoid_gate))).astype(jnp.bfloat16)
    grad_up = (grad_hidden * silu_gate).astype(jnp.bfloat16)
    block = FF // N_TENSOR

    def add_block(total, index):
        begin = (index * block).astype(jnp.int32)
        part_gate = lax.dynamic_slice_in_dim(grad_gate, begin, block, 1)
        part_up = lax.dynamic_slice_in_dim(grad_up, begin, block, 1)
        weight_gate = lax.dynamic_slice_in_dim(w_gate, begin, block, 1)
        weight_up = lax.dynamic_slice_in_dim(w_up, begin, block, 1)
        partial_value = (contract_last(part_gate, weight_gate) + contract_last(part_up, weight_up)).astype(jnp.bfloat16)
        partial_value = lax.optimization_barrier(partial_value)
        return (total + partial_value.astype(jnp.float32), None)
    summed, _ = lax.scan(add_block, jnp.zeros((TOKENS, D), jnp.float32), jnp.arange(N_TENSOR, dtype=jnp.int32))
    grad_input = summed.astype(jnp.bfloat16)
    table_ff = sign_table(buckets_ff, signs_ff)
    table_model = sign_table(buckets_d, signs_d)
    hidden_sketch = jnp.dot(hidden, table_ff, preferred_element_type=jnp.float32)
    grad_sketch = jnp.dot(d_live, table_model, preferred_element_type=jnp.float32)
    weighted = (member[:, :, None] * hidden_sketch[:, None, :]).reshape(TOKENS, EXAMPLES * SK)
    sketch = lax.dot_general(weighted, grad_sketch, (((0,), (0,)), ((), ())), precision=lax.Precision.HIGHEST, preferred_element_type=jnp.float32)
    sketch = sketch.reshape(EXAMPLES, SK * SK).astype(jnp.bfloat16)
    sketch_val = sketch.astype(jnp.float32)
    squares = lax.optimization_barrier(jnp.sum(sketch_val * sketch_val, axis=1))
    raw_scores = lax.dot_general(queries, sketch, (((1,), (1,)), ((), ())), preferred_element_type=jnp.float32)
    scores = raw_scores * lax.rsqrt(squares + 1e-06)[None, :]
    return (grad_input, scores)
```

```python
import jax
import jax.numpy as jnp
from jax import lax
from jax.sharding import PartitionSpec as P

SK = 256


def sign_table(buckets, signs):
    hits = buckets[:, None] == jnp.arange(SK, dtype=jnp.int32)[None, :]
    values = (2 * signs - 1).astype(jnp.float32)[:, None]
    return jnp.where(hits, values, jnp.float32(0.0)).astype(jnp.bfloat16)


def contract_last(left, right):
    return lax.dot_general(
        left, right, (((1,), (1,)), ((), ())), preferred_element_type=jnp.float32
    )


def example_pairs(left, right, member, starts, span):
    results = []
    for example in range(member.shape[1]):
        rows_left = lax.dynamic_slice_in_dim(left, starts[example], span, 0)
        rows_right = lax.dynamic_slice_in_dim(right, starts[example], span, 0)
        inside = lax.dynamic_slice_in_dim(member[:, example], starts[example], span, 0)
        results.append(
            lax.dot_general(
                rows_left * inside[:, None],
                rows_right,
                (((0,), (0,)), ((), ())),
                precision=lax.Precision.HIGHEST,
                preferred_element_type=jnp.float32,
            )
        )
    return jnp.stack(results, axis=0)


def swap_dp(value, bit):
    count = lax.axis_size("dp")
    return lax.ppermute(value, "dp", [(k, k ^ bit) for k in range(count)])


def swap_groups(value):
    return lax.ppermute(value, "groups", [(0, 1), (1, 0)])


def after(value, earlier):
    return lax.optimization_barrier((value, *earlier))[0]


def spread(blocks, done):
    group = lax.axis_index("groups")
    half = blocks[0].shape[1] // 2
    sides, nears, others = [], [], []
    for block in blocks:
        mine = lax.dynamic_slice_in_dim(block, group * half, half, 1)
        nears.append(swap_dp(after(mine, done[2]), 2))
    for block in blocks:
        sides.append(swap_dp(after(block, done[1]), 1))
    nears = [after(near, done[1]) for near in nears]
    others = [after(swap_groups(near), done[0]) for near in nears]

    def join(first, second):
        low = jnp.where(group == 0, first, second)
        high = jnp.where(group == 0, second, first)
        return jnp.concatenate([low, high], axis=1)

    results = []
    for block, side, near, other in zip(blocks, sides, nears, others):
        far = join(near, other)
        far_side = join(swap_dp(near, 1), swap_dp(other, 1))
        results.append([block, side, far, far_side])
    return results


def in_order(parts):
    k = lax.axis_index("dp")
    odd, far = (k % 2) == 1, k >= 2
    a, b, c, d = parts
    a, b = jnp.where(odd, b, a), jnp.where(odd, a, b)
    c, d = jnp.where(odd, d, c), jnp.where(odd, c, d)
    return [
        jnp.where(far, c, a),
        jnp.where(far, d, b),
        jnp.where(far, a, c),
        jnp.where(far, b, d),
    ]

DOWN_PIECES = 4
UP_TENTHS = (2, 2, 2, 2, 1, 1)


def local(
    gate_pre,
    up_pre,
    d_out,
    lengths,
    w_gate,
    w_up,
    w_down,
    buckets_ff,
    signs_ff,
    buckets_d,
    signs_d,
    queries,
):
    tok_count = gate_pre.shape[0]
    ex_count = lengths.shape[0]
    finish = jnp.cumsum(lengths)
    starts = finish - lengths
    row_ids = jnp.arange(tok_count, dtype=jnp.int32)[:, None]
    member = ((row_ids >= starts[None, :]) & (row_ids < finish[None, :])).astype(jnp.float32)
    live_rows = jnp.sum(member, axis=1)
    d_full = lax.all_gather(d_out, "tensor", axis=1, tiled=True)
    d_live = jnp.where(live_rows[:, None] > 0, d_full, jnp.zeros_like(d_full))
    columns = w_down.shape[1]
    k = lax.axis_index("dp")
    d_blocks = [
        lax.dynamic_slice_in_dim(d_live, (k ^ r) * columns, columns, 1) for r in range(4)
    ]
    pieces = []
    done = [(), (), ()]
    rows = w_down.shape[0] // DOWN_PIECES
    for p in range(DOWN_PIECES):
        (blocks,) = spread([w_down[None, p * rows : (p + 1) * rows]], done)
        total = contract_last(d_blocks[0], blocks[0][0])
        for r in range(1, 4):
            total = total + contract_last(d_blocks[r], blocks[r][0])
        pieces.append(total)
        done = [(total,)] + done[:2]
    grad_hidden = jnp.concatenate(pieces, axis=1)
    gate_val = gate_pre.astype(jnp.float32)
    up_val = up_pre.astype(jnp.float32)
    sigmoid_gate = jax.nn.sigmoid(gate_val)
    silu_gate = gate_val * sigmoid_gate
    hidden = (silu_gate * up_val).astype(jnp.bfloat16)
    grad_gate = (
        grad_hidden * up_val * sigmoid_gate * (1.0 + gate_val * (1.0 - sigmoid_gate))
    ).astype(jnp.bfloat16)
    grad_up = (grad_hidden * silu_gate).astype(jnp.bfloat16)
    table_ff = sign_table(buckets_ff, signs_ff)
    table_model = sign_table(buckets_d, signs_d)
    hidden_sketch = jnp.dot(hidden, table_ff, preferred_element_type=jnp.float32)
    grad_sketch = jnp.dot(d_live, table_model, preferred_element_type=jnp.float32)
    bucket_rows = SK // lax.axis_size("tensor")
    span = tok_count // 4
    summed_sketch = lax.psum_scatter(hidden_sketch, "tensor", scatter_dimension=1, tiled=True)
    sketch = example_pairs(summed_sketch, grad_sketch, member, starts, span)
    sketch = sketch.reshape(ex_count, bucket_rows * SK)
    sketch_low = sketch.astype(jnp.bfloat16)
    all_sketches = lax.all_gather(sketch_low, "dp", axis=0, tiled=True)
    raw_scores = contract_last(queries, all_sketches)
    sketch_val = all_sketches.astype(jnp.float32)
    squares = jnp.sum(sketch_val * sketch_val, axis=1)
    raw_scores, squares = lax.psum((raw_scores, squares), "tensor")
    scores = raw_scores * lax.rsqrt(squares + 1e-06)[None, :]
    width = d_out.shape[1]
    outer = w_gate.shape[0] // width
    gate_rows = w_gate.reshape(outer, width, w_gate.shape[1])
    up_rows = w_up.reshape(outer, width, w_up.shape[1])
    finals = []
    begin = 0
    for p, tenths in enumerate(UP_TENTHS):
        step = width * tenths // 10
        picked = slice(begin, begin + step)
        begin += step
        gate_blocks, up_blocks = spread([gate_rows[:, picked], up_rows[:, picked]], done)
        parts = []
        for gate_block, up_block in zip(gate_blocks, up_blocks):
            flat = (outer * step, w_gate.shape[1])
            parts.append(
                (
                    contract_last(grad_gate, gate_block.reshape(flat))
                    + contract_last(grad_up, up_block.reshape(flat))
                ).astype(jnp.bfloat16)
            )
        part = jnp.concatenate(in_order(parts), axis=1)
        finals.append(lax.psum_scatter(part, "tensor", scatter_dimension=1, tiled=True))
        done = [(part,) if p != 1 else (part, scores)] + done[:2]
    grad_input = jnp.concatenate(finals, axis=1)
    return (grad_input, scores)


def solution(mesh):
    in_specs = (
        P(("groups", "dp"), "tensor"),
        P(("groups", "dp"), "tensor"),
        P(("groups", "dp"), "tensor"),
        P(("groups", "dp")),
        P("dp", "tensor"),
        P("dp", "tensor"),
        P("tensor", "dp"),
        P("tensor"),
        P("tensor"),
        P(),
        P(),
        P("dp", "tensor"),
    )
    out_specs = (P(("groups", "dp"), "tensor"), P(("groups", "dp"), None))
    return jax.shard_map(local, mesh=mesh, in_specs=in_specs, out_specs=out_specs, check_vma=False)
```
